32 devices in a mesh: grid: 4 (over z), snap: 8 (over y, x, core).
Axes of the slice: x: 2, y: 2, z: 4, core: 2. Of those that a mesh axis runs over, the one named last changes fastest.
Arguments:
- snapshots: bfloat16 [8192, 16384], P('grid', 'snap'), may hold values from -6 to 6
- test_matrix: bfloat16 [128, 8192], P(None, 'grid'), may hold values from -0.0625 to 0.0625
- leaf_pivots: int32 [8, 128], P('snap'), may hold values from 0 to 2047, as said below
- leaf_inverse: float32 [8, 128, 128], P('snap'), as said below
- merge_pivots: int32 [7, 128], replicated, may hold values from 0 to 255, as said below
- merge_inverse: float32 [7, 128, 128], replicated, as said below
- skeleton_ids: int32 [128], replicated, may hold values from 0 to 16383, as said below
Outputs:
- skeleton: bfloat16 [8192, 128], P('grid')
- coefficients: bfloat16 [128, 16384], P(None, 'snap')
The draws below stay inside these ranges and needn't reach their ends.
Inputs may be any that keep to these rules, and one draw needn't show every extreme that they name: `leaf_pivots`: each row holds 128 distinct column numbers. `merge_pivots`: each row holds 128 distinct numbers. `skeleton_ids`: the ids that the tree keeps at node 1: leaf b starts with b * 2048 + leaf_pivots[b], each node keeps positions merge_pivots[n - 1] of its children's lists side by side. `leaf_inverse`: upper triangular with a positive diagonal. `merge_inverse`: upper triangular with a positive diagonal.
All inputs are finite; a program needn't handle non-finite values.
Results may differ from the reference program's by a relative error of at most 0.001.
Values may be sent and summed in bfloat16 or wider, within the bound.
A program may use at most 64 MiB of HBM per device.

```python
import jax
import jax.numpy as jnp
import numpy as np
from jax import lax

RANK = 128
COLS_DEV = 2048
ROWS = 8192
COLS = 16384
BLOCKS = 8


def place_value(listing, target, slot):
    where_now = jnp.argmax(listing == target).astype(jnp.int32)
    moved = listing[slot]
    listing = listing.at[where_now].set(moved)
    return listing.at[slot].set(target)


def leaf_row(sub, block):
    first_key, second_key = jax.random.split(sub)
    listing = jax.random.permutation(first_key, COLS_DEV).astype(jnp.int32)
    target = jnp.where(block == 0, jnp.int32(0), jnp.where(block == BLOCKS - 1, jnp.int32(COLS_DEV - 1), listing[0]))
    listing = place_value(listing, target, 0)
    return jax.random.permutation(second_key, listing[:RANK]).astype(jnp.int32)


def merge_row(sub):
    first_key, second_key = jax.random.split(sub)
    listing = jax.random.permutation(first_key, 2 * RANK).astype(jnp.int32)
    listing = place_value(listing, jnp.int32(0), 0)
    listing = place_value(listing, jnp.int32(RANK), 1)
    listing = place_value(listing, jnp.int32(2 * RANK - 1), 2)
    return jax.random.permutation(second_key, listing[:RANK]).astype(jnp.int32)


def tree_lists(key):
    leaf_key = jax.random.fold_in(key, 11)
    merge_key = jax.random.fold_in(key, 23)
    leaf_lists = jax.vmap(leaf_row)(jax.random.split(leaf_key, BLOCKS), jnp.arange(BLOCKS, dtype=jnp.int32))
    merge_lists = jax.vmap(merge_row)(jax.random.split(merge_key, BLOCKS - 1))
    global_ids = jnp.arange(BLOCKS, dtype=jnp.int32)[:, None] * COLS_DEV + leaf_lists
    node_count = BLOCKS
    while node_count > 1:
        half_count = node_count // 2
        stacked = jnp.concatenate([global_ids[0::2], global_ids[1::2]], axis=1)
        global_ids = jnp.take_along_axis(stacked, merge_lists[half_count - 1:2 * half_count - 1], axis=1)
        node_count = half_count
    return (leaf_lists.astype(jnp.int32), merge_lists.astype(jnp.int32), global_ids[0].astype(jnp.int32))


def triangular(key, count):
    first_key, second_key = jax.random.split(key)
    scales = jnp.exp(jax.random.uniform(first_key, (count, RANK, 1), jnp.float32, jnp.log(0.3), jnp.log(1.0)))
    noise = jax.random.normal(second_key, (count, RANK, RANK), jnp.float32)
    upper = jnp.triu(noise, 1) * (0.4 / jnp.sqrt(jnp.float32(RANK)))
    return scales * (jnp.eye(RANK, dtype=jnp.float32)[None] + upper) / RANK


def draw_leaf_pivots(key, part):
    return tree_lists(key)[0]


def draw_merge_pivots(key, part):
    return tree_lists(key)[1]


def draw_skeleton_ids(key, part):
    return tree_lists(key)[2]


def draw_leaf_inverse(key, part):
    return triangular(jax.random.fold_in(key, 37), BLOCKS)


def draw_merge_inverse(key, part):
    return triangular(jax.random.fold_in(key, 41), BLOCKS - 1)


def shard_levels(rng, shape, shards, least, top_value):
    def one(position, parts):
        draws = jax.random.uniform(jax.random.fold_in(jax.random.fold_in(rng, 6), position), (parts,), jnp.float32, least / len(shards), top_value / len(shards))
        return jnp.repeat(jnp.exp(draws), shape[position] // parts).reshape((-1,) + (1,) * (len(shape) - position - 1))

    level = one(*shards[0])
    for cut in shards[1:]:
        level = level * one(*cut)
    return level


def scatter_about(stream_key, shape, spread, bound, pieces=(), kind=jnp.bfloat16):
    drawn = spread * jax.random.normal(stream_key, shape, jnp.float32)
    if pieces:
        drawn = drawn * shard_levels(stream_key, shape, pieces, -0.22, 0.18)
    return jnp.clip(drawn, -bound, bound).astype(kind)


def setup_inputs(seed: int = 0) -> dict:
    arg_keys = jax.random.split(jax.random.key(seed), 8)
    snapshots = scatter_about(arg_keys[0], (ROWS, COLS), 1.0, 6.0, ((0, 4), (1, 8)))
    test_matrix = scatter_about(arg_keys[1], (RANK, ROWS), ROWS ** -0.5, 0.0625, ((1, 4),))
    leaf_pivots = draw_leaf_pivots(jax.random.fold_in(arg_keys[7], 71), 0)
    leaf_inverse = draw_leaf_inverse(jax.random.fold_in(arg_keys[7], 71), 0)
    merge_pivots = draw_merge_pivots(jax.random.fold_in(arg_keys[7], 71), 0)
    merge_inverse = draw_merge_inverse(jax.random.fold_in(arg_keys[7], 71), 0)
    skeleton_ids = draw_skeleton_ids(jax.random.fold_in(arg_keys[7], 71), 0)
    return {"snapshots": snapshots, "test_matrix": test_matrix, "leaf_pivots": leaf_pivots, "leaf_inverse": leaf_inverse, "merge_pivots": merge_pivots, "merge_inverse": merge_inverse, "skeleton_ids": skeleton_ids}


PRECISE = lax.Precision.HIGHEST


def identify(stacked, pivots, inverse):
    picker = (jnp.arange(stacked.shape[1], dtype=jnp.int32)[:, None] == pivots[None, :]).astype(jnp.float32)
    kept_cols = jnp.dot(stacked, picker, precision=PRECISE)
    projected = jnp.dot(kept_cols.T, stacked, precision=PRECISE)
    coeffs = jnp.dot(inverse, projected, precision=PRECISE)
    chosen_mask = jnp.sum(picker, axis=1)
    coeffs = coeffs * (1.0 - chosen_mask)[None, :] + picker.T
    return kept_cols, coeffs


def reference(snapshots, test_matrix, leaf_pivots, leaf_inverse, merge_pivots, merge_inverse, skeleton_ids):
    def leaf_block(block):
        start = (block * COLS_DEV).astype(jnp.int32)
        columns = lax.dynamic_slice_in_dim(snapshots, start, COLS_DEV, 1)
        sketch = jnp.dot(test_matrix, columns, preferred_element_type=jnp.float32)
        return identify(sketch, leaf_pivots[block], leaf_inverse[block])

    candidates, leaf_coeffs = lax.map(leaf_block, jnp.arange(BLOCKS, dtype=jnp.int32))
    composed = jnp.broadcast_to(jnp.eye(RANK, dtype=jnp.float32), (BLOCKS, RANK, RANK))
    node_count = BLOCKS
    tree_level = 1
    block_ids = np.arange(BLOCKS)
    while node_count > 1:
        half_count = node_count // 2
        stacked = jnp.concatenate([candidates[0::2], candidates[1::2]], axis=2)
        candidates, node_coeffs = jax.vmap(identify)(
            stacked, merge_pivots[half_count - 1:2 * half_count - 1], merge_inverse[half_count - 1:2 * half_count - 1])
        node_index = block_ids >> tree_level
        side_index = (block_ids >> (tree_level - 1)) & 1
        split_coeffs = node_coeffs.reshape(half_count, RANK, 2, RANK)
        portion = split_coeffs[node_index, :, side_index, :]
        composed = jnp.einsum("bij,bjk->bik", portion, composed, precision=PRECISE)
        node_count = half_count
        tree_level = tree_level + 1
    blocks_out = jnp.einsum("bij,bjc->bic", composed, leaf_coeffs, precision=PRECISE).astype(jnp.bfloat16)
    coefficients = jnp.transpose(blocks_out, (1, 0, 2)).reshape(RANK, BLOCKS * COLS_DEV)
    skeleton = jnp.take(snapshots, skeleton_ids, axis=1)
    return skeleton, coefficients
```

```python
import functools

import jax
import jax.numpy as jnp
from jax import lax
from jax.experimental import pallas as pl
from jax.experimental.pallas import tpu as pltpu
from jax.sharding import PartitionSpec as P

PRECISE = lax.Precision.HIGHEST
F32, BF16, I32, I16 = jnp.float32, jnp.bfloat16, jnp.int32, jnp.int16
TILE = 256
LIMIT = 32000.0


def precise_dot(a, b):
    return jnp.dot(a, b, precision=PRECISE, preferred_element_type=F32)


def split3(x):
    hi = x.astype(BF16)
    rest = x - hi.astype(F32)
    mid = rest.astype(BF16)
    lo = (rest - mid.astype(F32)).astype(BF16)
    return hi, mid, lo


def kernel(
    n, m, s_ref, t_ref, lp_ref, li_ref, mp_ref, mi_ref, ids_ref,
    skel_out, coef_out,
    sv, oh, spart, srs, sfull, kpart, krs, kzag, kall, cands, pbuf, mx, scale, q, rin, lin, rsum,
    lsum, w_s, c_s,
    load_sem, k_send, k_recv, g_send, g_recv, a_send, a_recv, s_send, s_recv, f_send, f_recv,
    mx_send, mx_recv, r_send, r_recv, l_send, l_recv,
):
    z = lax.axis_index("grid")
    b = lax.axis_index("snap")
    rank = t_ref.shape[0]
    rows, cols = sv.shape
    row_tiles, chunks = rows // TILE, cols // TILE
    per_group = chunks // 2
    krows = rank // n
    srows = rows // m
    levels = m.bit_length() - 1

    def remote(src, dst, send, recv, axis, target):
        return pltpu.make_async_remote_copy(
            src_ref=src, dst_ref=dst, send_sem=send, recv_sem=recv,
            device_id={axis: target}, device_id_type=pl.DeviceIdType.MESH,
        )

    def load(i):
        part = pl.ds(pl.multiple_of(i * TILE, TILE), TILE)
        return pltpu.make_async_copy(s_ref.at[part], sv.at[part], load_sem.at[i])

    for i in range(row_tiles):
        load(i).start()

    barrier = pltpu.get_barrier_semaphore()
    z_peers = [lax.rem(z + o, n) for o in range(1, n)]
    b_peers = [lax.rem(b + o, m) for o in range(1, m)]
    for d in z_peers:
        pl.semaphore_signal(barrier, inc=1, device_id={"grid": d}, device_id_type=pl.DeviceIdType.MESH)
    for d in b_peers:
        pl.semaphore_signal(barrier, inc=1, device_id={"snap": d}, device_id_type=pl.DeviceIdType.MESH)

    @pl.when(z == 0)
    def _():
        rin[...] = jnp.zeros_like(rin)

    @pl.when(z == n - 1)
    def _():
        lin[...] = jnp.zeros_like(lin)

    for g in range(2):
        mx[g, z] = jnp.zeros(mx.shape[2:], F32)

    local_ids = ids_ref[...] - b * cols
    picks = jnp.concatenate([local_ids, lp_ref[...]], axis=1)

    def fill(i, carry):
        base = pl.multiple_of(i * TILE, TILE)
        place = lax.broadcasted_iota(I32, (TILE, 2 * rank), 0) + base
        oh[pl.ds(base, TILE), :] = (place == picks).astype(F32).astype(BF16)
        return carry

    lax.fori_loop(0, chunks, fill, 0)

    def pick(i, kept):
        part = pl.ds(pl.multiple_of(i * TILE, TILE), TILE)
        load(i).wait()
        got = jnp.dot(sv[part, :], oh[...], preferred_element_type=F32).astype(BF16)
        spart[part, :] = got[:, :rank]
        return kept + jnp.dot(t_ref[:, part], got[:, rank:], preferred_element_type=F32)

    kept = lax.fori_loop(0, row_tiles, pick, jnp.zeros((rank, rank), F32))
    kpart[...] = kept.reshape(n, krows, rank)
    pl.semaphore_wait(barrier, n + m - 2)

    def k_copy(d, slot):
        return remote(kpart.at[d], krs.at[slot], k_send.at[d], k_recv.at[slot], "grid", d)

    def g_copy(d, slot):
        return remote(kzag.at[slot], kzag.at[slot], g_send.at[d], g_recv.at[slot], "grid", d)

    def a_copy(d, slot):
        return remote(kall.at[slot], kall.at[slot], a_send.at[d], a_recv.at[slot], "snap", d)

    def block(i):
        return pl.ds(pl.multiple_of(i * srows, 16), srows)

    def s_copy(d, slot):
        return remote(spart.at[block(d)], srs.at[slot], s_send.at[d], s_recv.at[slot], "snap", d)

    def f_copy(d, slot):
        return remote(
            sfull.at[block(slot)], sfull.at[block(slot)], f_send.at[d], f_recv.at[slot], "snap", d)

    def mx_copy(g, d, slot):
        return remote(mx.at[g, slot], mx.at[g, slot], mx_send.at[g, d], mx_recv.at[g, slot], "grid", d)

    for d in z_peers:
        k_copy(d, z).start()
    for d in b_peers:
        s_copy(d, b).start()

    def sketch(g):
        def one(i, carry):
            c = g * per_group + i
            part = pl.ds(pl.multiple_of(c * TILE, TILE), TILE)
            value = jnp.dot(t_ref[...], sv[:, part], preferred_element_type=F32)
            pbuf[c] = value
            mx[g, z, pl.ds(i, 1), :] = jnp.max(jnp.abs(value), axis=0, keepdims=True)
            return carry

        lax.fori_loop(0, per_group, one, 0)
        for d in z_peers:
            mx_copy(g, d, z).start()

    def quantise(g):
        for d in z_peers:
            mx_copy(g, d, d).wait_recv()
        top = mx[g, 0]
        for i in range(1, n):
            top = top + mx[g, i]
        top = jnp.maximum(top, 1e-30)
        scale[g] = top * (1.0 / LIMIT)
        inv = LIMIT / top
        for i in range(per_group):
            c = g * per_group + i
            q[c] = jnp.floor(pbuf[c] * inv[i:i + 1, :] + 0.5).astype(I32).astype(I16)

    def right_copy(c):
        return remote(rsum.at[c], rin.at[c], r_send.at[c], r_recv.at[c], "grid", lax.rem(z + 1, n))

    def left_copy(c):
        return remote(lsum.at[c], lin.at[c], l_send.at[c], l_recv.at[c], "grid", lax.rem(z + n - 1, n))

    def added(x, y):
        return (x.astype(I32) + y.astype(I32)).astype(I16)

    def go_right(c):
        @pl.when(z > 0)
        def _():
            right_copy(c).wait_recv()

        @pl.when(z < n - 1)
        def _():
            rsum[c] = added(rin[c], q[c])
            right_copy(c).start()

    def go_left(c):
        @pl.when(z < n - 1)
        def _():
            left_copy(c).wait_recv()

        @pl.when(z > 0)
        def _():
            lsum[c] = added(lin[c], q[c])
            left_copy(c).start()

    def flow(step):
        @pl.when(z < n // 2)
        def _():
            if step < chunks:
                go_right(step)
            if step > 0:
                go_left(step - 1)

        @pl.when(z >= n // 2)
        def _():
            if step < chunks:
                go_left(step)
            if step > 0:
                go_right(step - 1)

    sketch(0)
    for d in z_peers:
        k_copy(d, d).wait_recv()
    krs[z] = kpart[z]
    total = krs[0]
    for i in range(1, n):
        total = total + krs[i]
    kzag[z] = total
    for d in z_peers:
        g_copy(d, z).start()
    quantise(0)
    flow(0)
    sketch(1)
    for d in z_peers:
        g_copy(d, d).wait_recv()
    kall[b] = kzag[...]
    for d in b_peers:
        a_copy(d, b).start()
    flow(1)
    flow(2)

    for d in b_peers:
        s_copy(d, d).wait_recv()
    acc = spart[block(b), :].astype(F32)
    for d in b_peers:
        acc = acc + srs[d].astype(F32)
    sfull[block(b), :] = acc.astype(BF16)
    for d in b_peers:
        f_copy(d, b).start()
    flow(3)
    quantise(1)
    flow(4)

    for d in b_peers:
        a_copy(d, d).wait_recv()
    starts = [0]
    for level in range(levels):
        starts.append(starts[-1] + (m >> level))
    for i in range(m):
        cands[i] = kall[i].reshape(rank, rank)
    next_flow = 5
    for level in range(levels):
        nodes = m >> (level + 1)
        for j in range(nodes):
            stacked = jnp.concatenate(
                [cands[starts[level] + 2 * j], cands[starts[level] + 2 * j + 1]], axis=1)
            row = nodes - 1 + j
            picker = (
                lax.broadcasted_iota(I32, (2 * rank, rank), 0) == mp_ref[row:row + 1, :]
            ).astype(F32).astype(BF16)
            three = jnp.dot(
                jnp.concatenate(split3(stacked), axis=0), picker, preferred_element_type=F32)
            cands[starts[level + 1] + j] = (
                three[:rank] + three[rank:2 * rank]) + three[2 * rank:]
        if next_flow <= chunks:
            flow(next_flow)
            next_flow += 1
    composed = None
    for level in range(levels):
        nodes = m >> (level + 1)
        j = b >> (level + 1)
        side = (b >> level) & 1
        chosen = cands[starts[level + 1] + j]
        child = cands[starts[level] + (b >> level)]
        row = nodes - 1 + j
        pivots = mp_ref[pl.ds(row, 1), :]
        picker_t = (
            lax.broadcasted_iota(I32, (rank, rank), 0) + side * rank == pivots
        ).astype(F32).T
        mask = jnp.sum(picker_t, axis=0, keepdims=True)
        inner = precise_dot(chosen.T, child)
        portion = precise_dot(mi_ref[row], inner) * (1.0 - mask) + picker_t
        composed = portion if composed is None else precise_dot(portion, composed)
        if next_flow <= chunks:
            flow(next_flow)
            next_flow += 1
    while next_flow <= chunks:
        flow(next_flow)
        next_flow += 1
    own = cands[b]
    weight = precise_dot(composed, precise_dot(li_ref[0], own.T))
    w_hi, w_mid, _ = split3(weight)
    w_s[...] = jnp.concatenate([w_hi, w_hi, w_mid, w_mid], axis=1)
    c_s[...] = composed.astype(BF16)

    pivot_col = jnp.broadcast_to(lp_ref[...].astype(F32), (rank, rank)).T[:, :1].astype(I32)
    for c in range(chunks):
        g, i = c // per_group, c % per_group
        hit = (lax.broadcasted_iota(I32, (rank, TILE), 1) + c * TILE == pivot_col).astype(F32)
        keep = 1.0 - jnp.sum(hit, axis=0, keepdims=True)
        sums = rin[c].astype(I32) + q[c].astype(I32) + lin[c].astype(I32)
        value = sums.astype(F32) * keep
        hi = value.astype(BF16)
        lo = (value - hi.astype(F32)).astype(BF16)
        mapped = jnp.dot(
            w_s[...], jnp.concatenate([hi, lo, hi, lo], axis=0), preferred_element_type=F32)
        unit = jnp.dot(c_s[...], hit.astype(BF16), preferred_element_type=F32)
        coef_out[:, c * TILE:(c + 1) * TILE] = (mapped * scale[g, i:i + 1, :] + unit).astype(BF16)

    for d in b_peers:
        f_copy(d, d).wait_recv()
    skel_out[...] = sfull[...]

    for d in z_peers:
        k_copy(d, z).wait_send()
        g_copy(d, z).wait_send()
        for g in range(2):
            mx_copy(g, d, z).wait_send()
    for d in b_peers:
        a_copy(d, b).wait_send()
        s_copy(d, b).wait_send()
        f_copy(d, b).wait_send()

    @pl.when(z < n - 1)
    def _():
        for c in range(chunks):
            right_copy(c).wait_send()

    @pl.when(z > 0)
    def _():
        for c in range(chunks):
            left_copy(c).wait_send()


def per_device(
    n, m, snapshots, test_matrix, leaf_pivots, leaf_inverse, merge_pivots, merge_inverse, skeleton_ids
):
    rank = test_matrix.shape[0]
    rows, cols = snapshots.shape
    chunks = cols // TILE
    krows, srows = rank // n, rows // m
    vmem = pl.BlockSpec(memory_space=pltpu.VMEM)
    dma = pltpu.SemaphoreType.DMA
    flow_shape = (chunks, rank, TILE)
    return pl.pallas_call(
        functools.partial(kernel, n, m),
        out_shape=(
            jax.ShapeDtypeStruct((rows, rank), BF16),
            jax.ShapeDtypeStruct((rank, cols), BF16),
        ),
        in_specs=[pl.BlockSpec(memory_space=pl.ANY)] + [vmem] * 6,
        out_specs=(vmem, vmem),
        scratch_shapes=[
            pltpu.VMEM((rows, cols), BF16),
            pltpu.VMEM((cols, 2 * rank), BF16),
            pltpu.VMEM((rows, rank), BF16),
            pltpu.VMEM((m, srows, rank), BF16),
            pltpu.VMEM((rows, rank), BF16),
            pltpu.VMEM((n, krows, rank), F32),
            pltpu.VMEM((n, krows, rank), F32),
            pltpu.VMEM((n, krows, rank), F32),
            pltpu.VMEM((m, n, krows, rank), F32),
            pltpu.VMEM((2 * m, rank, rank), F32),
            pltpu.VMEM(flow_shape, F32),
            pltpu.VMEM((2, n, chunks, TILE), F32),
            pltpu.VMEM((2, chunks, TILE), F32),
            pltpu.VMEM(flow_shape, I16),
            pltpu.VMEM(flow_shape, I16),
            pltpu.VMEM(flow_shape, I16),
            pltpu.VMEM(flow_shape, I16),
            pltpu.VMEM(flow_shape, I16),
            pltpu.VMEM((rank, 4 * rank), BF16),
            pltpu.VMEM((rank, rank), BF16),
            dma((rows // TILE,)),
            dma((n,)), dma((n,)), dma((n,)), dma((n,)),
            dma((m,)), dma((m,)), dma((m,)), dma((m,)), dma((m,)), dma((m,)),
            dma((2, n)), dma((2, n)),
            dma((chunks,)), dma((chunks,)), dma((chunks,)), dma((chunks,)),
        ],
        compiler_params=pltpu.CompilerParams(
            collective_id=0, has_side_effects=True, vmem_limit_bytes=48 * 2**20
        ),
    )(
        snapshots, test_matrix, leaf_pivots, leaf_inverse, merge_pivots, merge_inverse,
        skeleton_ids.reshape(1, rank),
    )


def solution(mesh):
    return jax.shard_map(
        functools.partial(per_device, mesh.shape["grid"], mesh.shape["snap"]),
        mesh=mesh,
        in_specs=(
            P("grid", "snap"),
            P(None, "grid"),
            P("snap", None),
            P("snap", None, None),
            P(),
            P(),
            P(),
        ),
        out_specs=(P("grid", None), P(None, "snap")),
        check_vma=False,
    )
```

```python
import functools

import jax
import jax.numpy as jnp
from jax import lax
from jax.experimental import pallas as pl
from jax.experimental.pallas import tpu as pltpu
from jax.sharding import PartitionSpec as P

PRECISE = lax.Precision.HIGHEST
F32, BF16, I32, I16 = jnp.float32, jnp.bfloat16, jnp.int32, jnp.int16
TILE = 256
LIMIT = 32000.0
LAG = 2


def precise_dot(a, b):
    return jnp.dot(a, b, precision=PRECISE, preferred_element_type=F32)


def split3(x):
    hi = x.astype(BF16)
    rest = x - hi.astype(F32)
    mid = rest.astype(BF16)
    lo = (rest - mid.astype(F32)).astype(BF16)
    return hi, mid, lo


def kernel(
    n, m, s_ref, t_hbm, lp_hbm, li_hbm, mp_hbm, mi_hbm, ids_hbm,
    skel_out, coef_out,
    t_ref, lp_ref, li_ref, mp_ref, mi_ref, ids_ref, small_sem,
    sv, oh, spart, srs, sfull, kpart, krs, kzag, kall, cands, pbuf, mx, scale, q, rin, lin, rsum,
    lsum, w_s, c_s,
    load_sem, k_send, k_recv, g_send, g_recv, a_send, a_recv, s_send, s_recv, f_send, f_recv,
    mx_send, mx_recv, r_send, r_recv, l_send, l_recv,
):
    z = lax.axis_index("grid")
    b = lax.axis_index("snap")
    rank = t_ref.shape[0]
    rows, cols = sv.shape
    row_tiles, chunks = rows // TILE, cols // TILE
    per_group = chunks // 2
    krows = rank // n
    srows = rows // m
    levels = m.bit_length() - 1

    def remote(src, dst, send, recv, axis, target):
        return pltpu.make_async_remote_copy(
            src_ref=src, dst_ref=dst, send_sem=send, recv_sem=recv,
            device_id={axis: target}, device_id_type=pl.DeviceIdType.MESH,
        )

    def load(i):
        part = pl.ds(pl.multiple_of(i * TILE, TILE), TILE)
        return pltpu.make_async_copy(s_ref.at[part], sv.at[part], load_sem.at[i])

    small = [
        pltpu.make_async_copy(src, dst, small_sem.at[i])
        for i, (src, dst) in enumerate([
            (ids_hbm, ids_ref), (lp_hbm, lp_ref), (t_hbm, t_ref), (mp_hbm, mp_ref),
            (li_hbm, li_ref), (mi_hbm, mi_ref)])
    ]
    for copy in small[:3]:
        copy.start()
    for i in range(row_tiles):
        load(i).start()
    for copy in small[3:]:
        copy.start()

    barrier = pltpu.get_barrier_semaphore()
    z_peers = [lax.rem(z + o, n) for o in range(1, n)]
    b_peers = [lax.rem(b + o, m) for o in range(1, m)]
    for d in z_peers:
        pl.semaphore_signal(barrier, inc=1, device_id={"grid": d}, device_id_type=pl.DeviceIdType.MESH)
    for d in b_peers:
        pl.semaphore_signal(barrier, inc=1, device_id={"snap": d}, device_id_type=pl.DeviceIdType.MESH)

    @pl.when(z == 0)
    def _():
        rin[...] = jnp.zeros_like(rin)

    @pl.when(z == n - 1)
    def _():
        lin[...] = jnp.zeros_like(lin)

    for g in range(2):
        mx[g, z] = jnp.zeros(mx.shape[2:], F32)

    for copy in small[:2]:
        copy.wait()
    local_ids = ids_ref[...] - b * cols
    picks = jnp.concatenate([local_ids, lp_ref[...]], axis=1)

    def fill(i, carry):
        base = pl.multiple_of(i * TILE, TILE)
        place = lax.broadcasted_iota(I32, (TILE, 2 * rank), 0) + base
        oh[pl.ds(base, TILE), :] = (place == picks).astype(F32).astype(BF16)
        return carry

    lax.fori_loop(0, chunks, fill, 0)
    small[2].wait()

    def pick(i, kept):
        part = pl.ds(pl.multiple_of(i * TILE, TILE), TILE)
        load(i).wait()
        got = jnp.dot(sv[part, :], oh[...], preferred_element_type=F32).astype(BF16)
        spart[part, :] = got[:, :rank]
        return kept + jnp.dot(t_ref[:, part], got[:, rank:], preferred_element_type=F32)

    kept = lax.fori_loop(0, row_tiles, pick, jnp.zeros((rank, rank), F32))
    kpart[...] = kept.reshape(n, krows, rank)
    pl.semaphore_wait(barrier, n + m - 2)

    def k_copy(d, slot):
        return remote(kpart.at[d], krs.at[slot], k_send.at[d], k_recv.at[slot], "grid", d)

    def g_copy(d, slot):
        return remote(kzag.at[slot], kzag.at[slot], g_send.at[d], g_recv.at[slot], "grid", d)

    def a_copy(d, slot):
        return remote(kall.at[slot], kall.at[slot], a_send.at[d], a_recv.at[slot], "snap", d)

    def block(i):
        return pl.ds(pl.multiple_of(i * srows, 16), srows)

    def s_copy(d, slot):
        return remote(spart.at[block(d)], srs.at[slot], s_send.at[d], s_recv.at[slot], "snap", d)

    def f_copy(d, slot):
        return remote(
            sfull.at[block(slot)], sfull.at[block(slot)], f_send.at[d], f_recv.at[slot], "snap", d)

    def mx_copy(g, d, slot):
        return remote(mx.at[g, slot], mx.at[g, slot], mx_send.at[g, d], mx_recv.at[g, slot], "grid", d)

    for d in z_peers:
        k_copy(d, z).start()
    for d in b_peers:
        s_copy(d, b).start()

    def sketch(g):
        def one(i, carry):
            c = g * per_group + i
            part = pl.ds(pl.multiple_of(c * TILE, TILE), TILE)
            value = jnp.dot(t_ref[...], sv[:, part], preferred_element_type=F32)
            pbuf[c] = value
            mx[g, z, pl.ds(i, 1), :] = jnp.max(jnp.abs(value), axis=0, keepdims=True)
            return carry

        lax.fori_loop(0, per_group, one, 0)
        for d in z_peers:
            mx_copy(g, d, z).start()

    def quantise(g):
        for d in z_peers:
            mx_copy(g, d, d).wait_recv()
        top = mx[g, 0]
        for i in range(1, n):
            top = top + mx[g, i]
        top = jnp.maximum(top, 1e-30)
        scale[g] = top * (1.0 / LIMIT)
        inv = LIMIT / top
        for i in range(per_group):
            c = g * per_group + i
            q[c] = jnp.floor(pbuf[c] * inv[i:i + 1, :] + 0.5).astype(I32).astype(I16)

    def right_copy(c):
        return remote(rsum.at[c], rin.at[c], r_send.at[c], r_recv.at[c], "grid", lax.rem(z + 1, n))

    def left_copy(c):
        return remote(lsum.at[c], lin.at[c], l_send.at[c], l_recv.at[c], "grid", lax.rem(z + n - 1, n))

    def added(x, y):
        return (x.astype(I32) + y.astype(I32)).astype(I16)

    def go_right(c):
        right_copy(c).wait_recv()
        rsum[c] = added(rin[c], q[c])
        right_copy(c).start()

    def go_left(c):
        left_copy(c).wait_recv()
        lsum[c] = added(lin[c], q[c])
        left_copy(c).start()

    def from_ends(g):
        for c in range(g * per_group, (g + 1) * per_group):
            @pl.when(z == 0)
            def _():
                rsum[c] = q[c]
                right_copy(c).start()

            @pl.when(z == n - 1)
            def _():
                lsum[c] = q[c]
                left_copy(c).start()

    def flow(step):
        @pl.when((z > 0) & (z < n // 2))
        def _():
            if step < chunks:
                go_right(step)
            if step >= LAG:
                go_left(step - LAG)

        @pl.when((z >= n // 2) & (z < n - 1))
        def _():
            if step < chunks:
                go_left(step)
            if step >= LAG:
                go_right(step - LAG)

    sketch(0)
    for d in z_peers:
        k_copy(d, d).wait_recv()
    krs[z] = kpart[z]
    total = krs[0]
    for i in range(1, n):
        total = total + krs[i]
    kzag[z] = total
    for d in z_peers:
        g_copy(d, z).start()
    quantise(0)
    from_ends(0)
    sketch(1)
    for d in z_peers:
        g_copy(d, d).wait_recv()
    kall[b] = kzag[...]
    for d in b_peers:
        a_copy(d, b).start()
    flow(0)
    quantise(1)
    from_ends(1)
    for step in range(1, 5):
        flow(step)

    for d in b_peers:
        s_copy(d, d).wait_recv()
    acc = spart[block(b), :].astype(F32)
    for d in b_peers:
        acc = acc + srs[d].astype(F32)
    sfull[block(b), :] = acc.astype(BF16)
    for d in b_peers:
        f_copy(d, b).start()
    flow(5)

    for d in b_peers:
        a_copy(d, d).wait_recv()
    starts = [0]
    for level in range(levels):
        starts.append(starts[-1] + (m >> level))
    for i in range(m):
        cands[i] = kall[i].reshape(rank, rank)
    next_flow = 6
    for copy in small[3:]:
        copy.wait()
    for level in range(levels):
        nodes = m >> (level + 1)
        for j in range(nodes):
            stacked = jnp.concatenate(
                [cands[starts[level] + 2 * j], cands[starts[level] + 2 * j + 1]], axis=1)
            row = nodes - 1 + j
            picker = (
                lax.broadcasted_iota(I32, (2 * rank, rank), 0) == mp_ref[row:row + 1, :]
            ).astype(F32).astype(BF16)
            three = jnp.dot(
                jnp.concatenate(split3(stacked), axis=0), picker, preferred_element_type=F32)
            cands[starts[level + 1] + j] = (
                three[:rank] + three[rank:2 * rank]) + three[2 * rank:]
        if next_flow < chunks + LAG:
            flow(next_flow)
            next_flow += 1
    composed = None
    for level in range(levels):
        nodes = m >> (level + 1)
        j = b >> (level + 1)
        side = (b >> level) & 1
        chosen = cands[starts[level + 1] + j]
        child = cands[starts[level] + (b >> level)]
        row = nodes - 1 + j
        pivots = mp_ref[pl.ds(row, 1), :]
        picker_t = (
            lax.broadcasted_iota(I32, (rank, rank), 0) + side * rank == pivots
        ).astype(F32).T
        mask = jnp.sum(picker_t, axis=0, keepdims=True)
        inner = precise_dot(chosen.T, child)
        portion = precise_dot(mi_ref[row], inner) * (1.0 - mask) + picker_t
        composed = portion if composed is None else precise_dot(portion, composed)
        if next_flow < chunks + LAG:
            flow(next_flow)
            next_flow += 1
    while next_flow < chunks + LAG:
        flow(next_flow)
        next_flow += 1
    own = cands[b]
    weight = precise_dot(composed, precise_dot(li_ref[0], own.T))
    w_hi, w_mid, _ = split3(weight)
    w_s[...] = jnp.concatenate([w_hi, w_hi, w_mid, w_mid], axis=1)
    c_s[...] = composed.astype(BF16)

    @pl.when(z == 0)
    def _():
        for c in range(chunks):
            left_copy(c).wait_recv()

    @pl.when(z == n - 1)
    def _():
        for c in range(chunks):
            right_copy(c).wait_recv()

    pivot_col = jnp.broadcast_to(lp_ref[...].astype(F32), (rank, rank)).T[:, :1].astype(I32)
    for c in range(chunks):
        g, i = c // per_group, c % per_group
        hit = (lax.broadcasted_iota(I32, (rank, TILE), 1) + c * TILE == pivot_col).astype(F32)
        keep = 1.0 - jnp.sum(hit, axis=0, keepdims=True)
        sums = rin[c].astype(I32) + q[c].astype(I32) + lin[c].astype(I32)
        value = sums.astype(F32) * keep
        hi = value.astype(BF16)
        lo = (value - hi.astype(F32)).astype(BF16)
        mapped = jnp.dot(
            w_s[...], jnp.concatenate([hi, lo, hi, lo], axis=0), preferred_element_type=F32)
        unit = jnp.dot(c_s[...], hit.astype(BF16), preferred_element_type=F32)
        coef_out[:, c * TILE:(c + 1) * TILE] = (mapped * scale[g, i:i + 1, :] + unit).astype(BF16)

    for d in b_peers:
        f_copy(d, d).wait_recv()
    skel_out[...] = sfull[...]

    for d in z_peers:
        k_copy(d, z).wait_send()
        g_copy(d, z).wait_send()
        for g in range(2):
            mx_copy(g, d, z).wait_send()
    for d in b_peers:
        a_copy(d, b).wait_send()
        s_copy(d, b).wait_send()
        f_copy(d, b).wait_send()

    @pl.when(z < n - 1)
    def _():
        for c in range(chunks):
            right_copy(c).wait_send()

    @pl.when(z > 0)
    def _():
        for c in range(chunks):
            left_copy(c).wait_send()


def per_device(
    n, m, snapshots, test_matrix, leaf_pivots, leaf_inverse, merge_pivots, merge_inverse, skeleton_ids
):
    rank = test_matrix.shape[0]
    rows, cols = snapshots.shape
    chunks = cols // TILE
    krows, srows = rank // n, rows // m
    vmem = pl.BlockSpec(memory_space=pltpu.VMEM)
    dma = pltpu.SemaphoreType.DMA
    flow_shape = (chunks, rank, TILE)
    return pl.pallas_call(
        functools.partial(kernel, n, m),
        out_shape=(
            jax.ShapeDtypeStruct((rows, rank), BF16),
            jax.ShapeDtypeStruct((rank, cols), BF16),
        ),
        in_specs=[pl.BlockSpec(memory_space=pl.ANY)] * 7,
        out_specs=(vmem, vmem),
        scratch_shapes=[
            pltpu.VMEM(test_matrix.shape, BF16),
            pltpu.VMEM(leaf_pivots.shape, I32),
            pltpu.VMEM(leaf_inverse.shape, F32),
            pltpu.VMEM(merge_pivots.shape, I32),
            pltpu.VMEM(merge_inverse.shape, F32),
            pltpu.VMEM((1, rank), I32),
            dma((6,)),
            pltpu.VMEM((rows, cols), BF16),
            pltpu.VMEM((cols, 2 * rank), BF16),
            pltpu.VMEM((rows, rank), BF16),
            pltpu.VMEM((m, srows, rank), BF16),
            pltpu.VMEM((rows, rank), BF16),
            pltpu.VMEM((n, krows, rank), F32),
            pltpu.VMEM((n, krows, rank), F32),
            pltpu.VMEM((n, krows, rank), F32),
            pltpu.VMEM((m, n, krows, rank), F32),
            pltpu.VMEM((2 * m, rank, rank), F32),
            pltpu.VMEM(flow_shape, F32),
            pltpu.VMEM((2, n, chunks, TILE), F32),
            pltpu.VMEM((2, chunks, TILE), F32),
            pltpu.VMEM(flow_shape, I16),
            pltpu.VMEM(flow_shape, I16),
            pltpu.VMEM(flow_shape, I16),
            pltpu.VMEM(flow_shape, I16),
            pltpu.VMEM(flow_shape, I16),
            pltpu.VMEM((rank, 4 * rank), BF16),
            pltpu.VMEM((rank, rank), BF16),
            dma((rows // TILE,)),
            dma((n,)), dma((n,)), dma((n,)), dma((n,)),
            dma((m,)), dma((m,)), dma((m,)), dma((m,)), dma((m,)), dma((m,)),
            dma((2, n)), dma((2, n)),
            dma((chunks,)), dma((chunks,)), dma((chunks,)), dma((chunks,)),
        ],
        compiler_params=pltpu.CompilerParams(
            collective_id=0, has_side_effects=True, vmem_limit_bytes=48 * 2**20
        ),
    )(
        snapshots, test_matrix, leaf_pivots, leaf_inverse, merge_pivots, merge_inverse,
        skeleton_ids.reshape(1, rank),
    )


def solution(mesh):
    return jax.shard_map(
        functools.partial(per_device, mesh.shape["grid"], mesh.shape["snap"]),
        mesh=mesh,
        in_specs=(
            P("grid", "snap"),
            P(None, "grid"),
            P("snap", None),
            P("snap", None, None),
            P(),
            P(),
            P(),
        ),
        out_specs=(P("grid", None), P(None, "snap")),
        check_vma=False,
    )
```

```python
import functools

import jax
import jax.numpy as jnp
from jax import lax
from jax.experimental import pallas as pl
from jax.experimental.pallas import tpu as pltpu
from jax.sharding import PartitionSpec as P

PRECISE = lax.Precision.HIGHEST
F32, BF16, I32, I16 = jnp.float32, jnp.bfloat16, jnp.int32, jnp.int16
TILE = 256
LIMIT = 32000.0
LAG = 2
GROUPS = 4


def precise_dot(a, b):
    return jnp.dot(a, b, precision=PRECISE, preferred_element_type=F32)


def split3(x):
    hi = x.astype(BF16)
    rest = x - hi.astype(F32)
    mid = rest.astype(BF16)
    lo = (rest - mid.astype(F32)).astype(BF16)
    return hi, mid, lo


def kernel(
    n, m, s_ref, t_hbm, lp_hbm, li_hbm, mp_hbm, mi_hbm, ids_hbm,
    skel_out, coef_out,
    t_ref, lp_ref, li_ref, mp_ref, mi_ref, ids_ref, small_sem,
    sv, oh, spart, lcols, shalf, srs, sfull, kpart, krs, kzag, kall, cpick, v_s, pbuf, mx, scale, q, rin, lin, rsum,
    lsum, w_s, c_s,
    load_sem, k_send, k_recv, g_send, g_recv, a_send, a_recv, h_send, h_recv, s_send, s_recv,
    f_send, f_recv,
    mx_send, mx_recv, r_send, r_recv, l_send, l_recv,
):
    z = lax.axis_index("grid")
    b = lax.axis_index("snap")
    rank = t_ref.shape[0]
    rows, cols = sv.shape
    row_tiles, chunks = rows // TILE, cols // TILE
    per_group = chunks // GROUPS
    krows = rank // n
    srows = rows // m
    levels = m.bit_length() - 1

    def remote(src, dst, send, recv, axis, target):
        return pltpu.make_async_remote_copy(
            src_ref=src, dst_ref=dst, send_sem=send, recv_sem=recv,
            device_id={axis: target}, device_id_type=pl.DeviceIdType.MESH,
        )

    def load(i):
        part = pl.ds(pl.multiple_of(i * TILE, TILE), TILE)
        return pltpu.make_async_copy(s_ref.at[part], sv.at[part], load_sem.at[i])

    small = [
        pltpu.make_async_copy(src, dst, small_sem.at[i])
        for i, (src, dst) in enumerate([
            (ids_hbm, ids_ref), (lp_hbm, lp_ref), (t_hbm, t_ref), (mp_hbm, mp_ref),
            (li_hbm, li_ref), (mi_hbm, mi_ref)])
    ]
    for copy in small[:3]:
        copy.start()
    for i in range(row_tiles):
        load(i).start()
    for copy in small[3:]:
        copy.start()

    barrier = pltpu.get_barrier_semaphore()
    z_peers = [lax.rem(z + o, n) for o in range(1, n)]
    b_peers = [lax.rem(b + o, m) for o in range(1, m)]
    for d in z_peers:
        pl.semaphore_signal(barrier, inc=1, device_id={"grid": d}, device_id_type=pl.DeviceIdType.MESH)
    for d in b_peers:
        pl.semaphore_signal(barrier, inc=1, device_id={"snap": d}, device_id_type=pl.DeviceIdType.MESH)

    @pl.when(z == 0)
    def _():
        rin[...] = jnp.zeros_like(rin)

    @pl.when(z == n - 1)
    def _():
        lin[...] = jnp.zeros_like(lin)

    for g in range(GROUPS):
        mx[g, z] = jnp.zeros(mx.shape[2:], F32)

    for copy in small[:2]:
        copy.wait()
    local_ids = ids_ref[...] - b * cols
    picks = jnp.concatenate([local_ids, lp_ref[...]], axis=1)

    def fill(i, carry):
        base = pl.multiple_of(i * TILE, TILE)
        place = lax.broadcasted_iota(I32, (TILE, 2 * rank), 0) + base
        oh[pl.ds(base, TILE), :] = (place == picks).astype(F32).astype(BF16)
        return carry

    lax.fori_loop(0, chunks, fill, 0)
    small[2].wait()

    wide = 2 * TILE
    for i in range(rows // wide):
        part = pl.ds(i * wide, wide)
        load(2 * i).wait()
        load(2 * i + 1).wait()
        got = jnp.dot(sv[part, :], oh[...], preferred_element_type=F32).astype(BF16)
        spart[part, :] = got[:, :rank]
        lcols[part, :] = got[:, rank:]
    kept = jnp.dot(t_ref[...], lcols[...], preferred_element_type=F32)
    kpart[...] = kept.reshape(n, krows, rank)
    pl.semaphore_wait(barrier, n + m - 2)

    def k_copy(d, slot):
        return remote(kpart.at[d], krs.at[slot], k_send.at[d], k_recv.at[slot], "grid", d)

    def g_copy(d, slot):
        return remote(kzag.at[slot], kzag.at[slot], g_send.at[d], g_recv.at[slot], "grid", d)

    core, chip, half = b & 1, b >> 1, m // 2
    mate = b ^ 1
    chip_peers = [lax.rem(chip + o, half) * 2 + core for o in range(1, half)]

    def a_copy(d, slot):
        return remote(kall.at[slot], kall.at[slot], a_send.at[d], a_recv.at[slot], "snap", d)

    def a_forward(slot):
        return remote(kall.at[slot], kall.at[slot], a_send.at[slot ^ 1], a_recv.at[slot], "snap", mate)

    def block(d):
        place = (d & 1) * half + (d >> 1)
        return pl.ds(pl.multiple_of(place * srows, 16), srows)

    def side(which):
        return pl.ds(pl.multiple_of(which * half * srows, 16), half * srows)

    def h_copy(which):
        return remote(spart.at[side(which)], shalf, h_send, h_recv, "snap", mate)

    def s_copy(d, slot):
        return remote(
            spart.at[block(d)], srs.at[slot >> 1], s_send.at[d >> 1], s_recv.at[slot >> 1], "snap", d)

    def f_copy(d, slot):
        return remote(
            sfull.at[block(slot)], sfull.at[block(slot)], f_send.at[d], f_recv.at[slot], "snap", d)

    def f_forward(slot):
        return remote(
            sfull.at[block(slot)], sfull.at[block(slot)], f_send.at[slot ^ 1], f_recv.at[slot],
            "snap", mate)

    def mx_copy(g, d, slot):
        return remote(mx.at[g, slot], mx.at[g, slot], mx_send.at[g, d], mx_recv.at[g, slot], "grid", d)

    for d in z_peers:
        k_copy(d, z).start()
    h_copy(1 - core).start()

    def sketch(g):
        for i in range(per_group):
            c = g * per_group + i
            value = jnp.dot(
                t_ref[...], sv[:, c * TILE:(c + 1) * TILE], preferred_element_type=F32)
            pbuf[c] = value
            mx[g, z, i:i + 1, :] = jnp.max(jnp.abs(value), axis=0, keepdims=True)
        for d in z_peers:
            mx_copy(g, d, z).start()

    def quantise(g):
        for d in z_peers:
            mx_copy(g, d, d).wait_recv()
        top = mx[g, 0]
        for i in range(1, n):
            top = top + mx[g, i]
        top = jnp.maximum(top, 1e-30)
        scale[g] = top * (1.0 / LIMIT)
        inv = LIMIT / top
        for i in range(per_group):
            c = g * per_group + i
            q[c] = jnp.floor(pbuf[c] * inv[i:i + 1, :] + 0.5).astype(I32).astype(I16)

    def right_copy(c):
        return remote(rsum.at[c], rin.at[c], r_send.at[c], r_recv.at[c], "grid", lax.rem(z + 1, n))

    def left_copy(c):
        return remote(lsum.at[c], lin.at[c], l_send.at[c], l_recv.at[c], "grid", lax.rem(z + n - 1, n))

    def added(x, y):
        return (x.astype(I32) + y.astype(I32)).astype(I16)

    def go_right(c):
        right_copy(c).wait_recv()
        rsum[c] = added(rin[c], q[c])
        right_copy(c).start()

    def go_left(c):
        left_copy(c).wait_recv()
        lsum[c] = added(lin[c], q[c])
        left_copy(c).start()

    def from_ends(g):
        for c in range(g * per_group, (g + 1) * per_group):
            @pl.when(z == 0)
            def _():
                rsum[c] = q[c]
                right_copy(c).start()

            @pl.when(z == n - 1)
            def _():
                lsum[c] = q[c]
                left_copy(c).start()

    def flow(step):
        @pl.when((z > 0) & (z < n // 2))
        def _():
            if step < chunks:
                go_right(step)
            if step >= LAG:
                go_left(step - LAG)

        @pl.when((z >= n // 2) & (z < n - 1))
        def _():
            if step < chunks:
                go_left(step)
            if step >= LAG:
                go_right(step - LAG)

    def skeleton_half():
        h_copy(core).wait_recv()
        h_copy(1 - core).wait_send()
        mine = side(core)
        spart[mine, :] = (spart[mine, :].astype(F32) + shalf[...].astype(F32)).astype(BF16)
        for d in chip_peers:
            s_copy(d, b).start()

    def skeleton_block():
        acc = spart[block(b), :].astype(F32)
        for d in chip_peers:
            s_copy(d, d).wait_recv()
            acc = acc + srs[d >> 1].astype(F32)
        sfull[block(b), :] = acc.astype(BF16)
        for d in chip_peers + [mate]:
            f_copy(d, b).start()

    def skeleton_forward():
        for d in chip_peers:
            f_copy(d, d).wait_recv()
            f_forward(d).start()

    def selections():
        def row_of(level, j):
            return mp_ref[pl.ds((m >> (level + 1)) - 1 + j, 1), :]

        ids = [j * 2 * rank + mp_ref[m // 2 - 1 + j:m // 2 + j, :] for j in range(m // 2)]
        for level in range(levels):
            if level:
                merged = []
                for j in range(len(ids) // 2):
                    both = jnp.concatenate([ids[2 * j], ids[2 * j + 1]], axis=1).astype(F32)
                    picker = (
                        lax.broadcasted_iota(I32, (2 * rank, rank), 0)
                        == mp_ref[len(ids) // 2 - 1 + j:len(ids) // 2 + j, :]
                    ).astype(F32)
                    found = precise_dot(jnp.broadcast_to(both, (8, 2 * rank)), picker)
                    merged.append(jnp.floor(found[:1] + 0.5).astype(I32))
                ids = merged
            mine = ids[0]
            for j in range(1, len(ids)):
                mine = jnp.where(b >> (level + 1) == j, ids[j], mine)
            for i in range(m):
                place = lax.broadcasted_iota(I32, (rank, rank), 0) + i * rank
                cpick[i, :, level * rank:(level + 1) * rank] = (
                    place == mine).astype(F32).astype(BF16)

    def tree():
        three = None
        for i in range(m):
            parts = jnp.concatenate(split3(kall[i].reshape(rank, rank)), axis=0)
            found = jnp.dot(parts, cpick[i], preferred_element_type=F32)
            three = found if three is None else three + found
        chosen = (three[:rank] + three[rank:2 * rank]) + three[2 * rank:]
        path = [kall[b].reshape(rank, rank)]
        for level in range(levels):
            path.append(chosen[:, level * rank:(level + 1) * rank])
        portions = []
        for level in range(levels):
            row = (m >> (level + 1)) - 1 + (b >> (level + 1))
            picker_t = (
                lax.broadcasted_iota(I32, (rank, rank), 0) + ((b >> level) & 1) * rank
                == mp_ref[pl.ds(row, 1), :]
            ).astype(F32).T
            mask = jnp.sum(picker_t, axis=0, keepdims=True)
            inner = precise_dot(path[level + 1].T, path[level])
            portions.append(precise_dot(mi_ref[row], inner) * (1.0 - mask) + picker_t)
        top = portions[-1]
        for level in range(levels - 2, 0, -1):
            top = precise_dot(top, portions[level])
        first = precise_dot(portions[0], v_s[...])
        composed = precise_dot(top, portions[0]) if levels > 1 else top
        weight = precise_dot(top, first) if levels > 1 else first
        w_hi, w_mid, _ = split3(weight)
        w_s[...] = jnp.concatenate([w_hi, w_hi, w_mid, w_mid], axis=1)
        c_s[...] = composed.astype(BF16)

    def finish(c):
        @pl.when(z == 0)
        def _():
            left_copy(c).wait_recv()

        @pl.when(z == n - 1)
        def _():
            right_copy(c).wait_recv()

        g, i = c // per_group, c % per_group
        hit = (lax.broadcasted_iota(I32, (rank, TILE), 1) + c * TILE == pivot_col).astype(F32)
        keep = 1.0 - jnp.sum(hit, axis=0, keepdims=True)
        sums = rin[c].astype(I32) + q[c].astype(I32) + lin[c].astype(I32)
        value = sums.astype(F32) * keep
        hi = value.astype(BF16)
        lo = (value - hi.astype(F32)).astype(BF16)
        mapped = jnp.dot(
            w_s[...], jnp.concatenate([hi, lo, hi, lo], axis=0), preferred_element_type=F32)
        unit = jnp.dot(c_s[...], hit.astype(BF16), preferred_element_type=F32)
        coef_out[:, c * TILE:(c + 1) * TILE] = (mapped * scale[g, i:i + 1, :] + unit).astype(BF16)

    sketch(0)
    sketch(1)
    for d in z_peers:
        k_copy(d, d).wait_recv()
    krs[z] = kpart[z]
    total = krs[0]
    for i in range(1, n):
        total = total + krs[i]
    kzag[z] = total
    for d in z_peers:
        g_copy(d, z).start()
    quantise(0)
    from_ends(0)
    sketch(2)
    quantise(1)
    from_ends(1)
    sketch(3)
    for copy in small[3:]:
        copy.wait()
    for d in z_peers:
        g_copy(d, d).wait_recv()
    kall[b] = kzag[...]
    for d in chip_peers + [mate]:
        a_copy(d, b).start()
    flow(0)
    quantise(2)
    from_ends(2)
    flow(1)
    quantise(3)
    from_ends(3)
    skeleton_half()
    flow(2)
    selections()
    v_s[...] = precise_dot(li_ref[0], kzag[...].reshape(rank, rank).T)
    pivot_col = jnp.broadcast_to(lp_ref[...].astype(F32), (rank, rank)).T[:, :1].astype(I32)
    flow(3)
    for d in chip_peers:
        a_copy(d, d).wait_recv()
        a_forward(d).start()
    flow(4)
    skeleton_block()
    flow(5)
    a_copy(mate, mate).wait_recv()
    for d in chip_peers:
        a_copy(d, d ^ 1).wait_recv()
    tree()
    for step in range(6, chunks + LAG):
        flow(step)
        if step == 6:
            skeleton_forward()
            for c in range(step - LAG):
                finish(c)
        finish(step - LAG)
    f_copy(mate, mate).wait_recv()
    for d in chip_peers:
        f_copy(d, d ^ 1).wait_recv()
    skel_out[...] = sfull[...]

    for d in z_peers:
        k_copy(d, z).wait_send()
        g_copy(d, z).wait_send()
        for g in range(GROUPS):
            mx_copy(g, d, z).wait_send()
    for d in chip_peers:
        s_copy(d, b).wait_send()
        a_copy(d, b).wait_send()
        f_copy(d, b).wait_send()
        a_forward(d).wait_send()
        f_forward(d).wait_send()
    a_copy(mate, b).wait_send()
    f_copy(mate, b).wait_send()

    @pl.when(z < n - 1)
    def _():
        for c in range(chunks):
            right_copy(c).wait_send()

    @pl.when(z > 0)
    def _():
        for c in range(chunks):
            left_copy(c).wait_send()


def per_device(
    n, m, snapshots, test_matrix, leaf_pivots, leaf_inverse, merge_pivots, merge_inverse, skeleton_ids
):
    rank = test_matrix.shape[0]
    rows, cols = snapshots.shape
    chunks = cols // TILE
    krows, srows = rank // n, rows // m
    vmem = pl.BlockSpec(memory_space=pltpu.VMEM)
    dma = pltpu.SemaphoreType.DMA
    flow_shape = (chunks, rank, TILE)
    return pl.pallas_call(
        functools.partial(kernel, n, m),
        out_shape=(
            jax.ShapeDtypeStruct((rows, rank), BF16),
            jax.ShapeDtypeStruct((rank, cols), BF16),
        ),
        in_specs=[pl.BlockSpec(memory_space=pl.ANY)] * 7,
        out_specs=(vmem, vmem),
        scratch_shapes=[
            pltpu.VMEM(test_matrix.shape, BF16),
            pltpu.VMEM(leaf_pivots.shape, I32),
            pltpu.VMEM(leaf_inverse.shape, F32),
            pltpu.VMEM(merge_pivots.shape, I32),
            pltpu.VMEM(merge_inverse.shape, F32),
            pltpu.VMEM((1, rank), I32),
            dma((6,)),
            pltpu.VMEM((rows, cols), BF16),
            pltpu.VMEM((cols, 2 * rank), BF16),
            pltpu.VMEM((rows, rank), BF16),
            pltpu.VMEM((rows, rank), BF16),
            pltpu.VMEM((rows // 2, rank), BF16),
            pltpu.VMEM((m // 2, srows, rank), BF16),
            pltpu.VMEM((rows, rank), BF16),
            pltpu.VMEM((n, krows, rank), F32),
            pltpu.VMEM((n, krows, rank), F32),
            pltpu.VMEM((n, krows, rank), F32),
            pltpu.VMEM((m, n, krows, rank), F32),
            pltpu.VMEM((m, rank, rank * (m.bit_length() - 1)), BF16),
            pltpu.VMEM((rank, rank), F32),
            pltpu.VMEM(flow_shape, F32),
            pltpu.VMEM((GROUPS, n, 8, TILE), F32),
            pltpu.VMEM((GROUPS, 8, TILE), F32),
            pltpu.VMEM(flow_shape, I16),
            pltpu.VMEM(flow_shape, I16),
            pltpu.VMEM(flow_shape, I16),
            pltpu.VMEM(flow_shape, I16),
            pltpu.VMEM(flow_shape, I16),
            pltpu.VMEM((rank, 4 * rank), BF16),
            pltpu.VMEM((rank, rank), BF16),
            dma((rows // TILE,)),
            dma((n,)), dma((n,)), dma((n,)), dma((n,)),
            dma((m,)), dma((m,)), dma, dma, dma((m // 2,)), dma((m // 2,)), dma((m,)), dma((m,)),
            dma((GROUPS, n)), dma((GROUPS, n)),
            dma((chunks,)), dma((chunks,)), dma((chunks,)), dma((chunks,)),
        ],
        compiler_params=pltpu.CompilerParams(
            collective_id=0, has_side_effects=True, vmem_limit_bytes=64 * 2**20
        ),
    )(
        snapshots, test_matrix, leaf_pivots, leaf_inverse, merge_pivots, merge_inverse,
        skeleton_ids.reshape(1, rank),
    )


def solution(mesh):
    return jax.shard_map(
        functools.partial(per_device, mesh.shape["grid"], mesh.shape["snap"]),
        mesh=mesh,
        in_specs=(
            P("grid", "snap"),
            P(None, "grid"),
            P("snap", None),
            P("snap", None, None),
            P(),
            P(),
            P(),
        ),
        out_specs=(P("grid", None), P(None, "snap")),
        check_vma=False,
    )
```

```python
import functools

import jax
import jax.numpy as jnp
from jax import lax
from jax.experimental import pallas as pl
from jax.experimental.pallas import tpu as pltpu
from jax.sharding import PartitionSpec as P

PRECISE = lax.Precision.HIGHEST
F32, BF16, I32, I16 = jnp.float32, jnp.bfloat16, jnp.int32, jnp.int16
TILE = 256
LIMIT = 32000.0
LAG = 2
GROUPS = 4


def precise_dot(a, b):
    return jnp.dot(a, b, precision=PRECISE, preferred_element_type=F32)


def split3(x):
    hi = x.astype(BF16)
    rest = x - hi.astype(F32)
    mid = rest.astype(BF16)
    lo = (rest - mid.astype(F32)).astype(BF16)
    return hi, mid, lo


def kernel(
    n, m, s_ref, t_hbm, lp_hbm, li_hbm, mp_hbm, mi_hbm, ids_hbm,
    skel_out, coef_out,
    t_ref, lp_ref, li_ref, mp_ref, mi_ref, ids_ref, small_sem,
    sv, oh, spart, lcols, shalf, srs, sfull, kpart, krs, kzag, kall, cpick, kparts, inverse, v_s, pbuf, mx, scale, q, rin, lin, rsum,
    lsum, w_s, c_s,
    load_sem, k_send, k_recv, g_send, g_recv, a_send, a_recv, h_send, h_recv, s_send, s_recv,
    f_send, f_recv,
    mx_send, mx_recv, r_send, r_recv, l_send, l_recv,
):
    z = lax.axis_index("grid")
    b = lax.axis_index("snap")
    rank = t_ref.shape[0]
    rows, cols = sv.shape
    row_tiles, chunks = rows // TILE, cols // TILE
    per_group = chunks // GROUPS
    krows = rank // n
    srows = rows // m
    levels = m.bit_length() - 1

    def remote(src, dst, send, recv, axis, target):
        return pltpu.make_async_remote_copy(
            src_ref=src, dst_ref=dst, send_sem=send, recv_sem=recv,
            device_id={axis: target}, device_id_type=pl.DeviceIdType.MESH,
        )

    def load(i):
        part = pl.ds(pl.multiple_of(i * TILE, TILE), TILE)
        return pltpu.make_async_copy(s_ref.at[part], sv.at[part], load_sem.at[i])

    small = [
        pltpu.make_async_copy(src, dst, small_sem.at[i])
        for i, (src, dst) in enumerate([
            (ids_hbm, ids_ref), (lp_hbm, lp_ref), (t_hbm, t_ref), (mp_hbm, mp_ref),
            (li_hbm, li_ref), (mi_hbm, mi_ref)])
    ]
    for copy in small[:3]:
        copy.start()
    for i in range(row_tiles):
        load(i).start()
    for copy in small[3:]:
        copy.start()

    barrier = pltpu.get_barrier_semaphore()
    z_peers = [lax.rem(z + o, n) for o in range(1, n)]
    b_peers = [lax.rem(b + o, m) for o in range(1, m)]
    for d in z_peers:
        pl.semaphore_signal(barrier, inc=1, device_id={"grid": d}, device_id_type=pl.DeviceIdType.MESH)
    for d in b_peers:
        pl.semaphore_signal(barrier, inc=1, device_id={"snap": d}, device_id_type=pl.DeviceIdType.MESH)

    @pl.when(z == 0)
    def _():
        rin[...] = jnp.zeros_like(rin)

    @pl.when(z == n - 1)
    def _():
        lin[...] = jnp.zeros_like(lin)

    for g in range(GROUPS):
        mx[g, z] = jnp.zeros(mx.shape[2:], F32)

    for copy in small[:2]:
        copy.wait()
    local_ids = ids_ref[...] - b * cols
    picks = jnp.concatenate([local_ids, lp_ref[...]], axis=1)

    def fill(i, carry):
        base = pl.multiple_of(i * TILE, TILE)
        place = lax.broadcasted_iota(I32, (TILE, 2 * rank), 0) + base
        oh[pl.ds(base, TILE), :] = (place == picks).astype(F32).astype(BF16)
        return carry

    lax.fori_loop(0, chunks, fill, 0)
    small[2].wait()

    def pick(i, carry):
        part = pl.ds(pl.multiple_of(i * TILE, TILE), TILE)
        load(i).wait()
        got = jnp.dot(sv[part, :], oh[...], preferred_element_type=F32).astype(BF16)
        spart[part, :] = got[:, :rank]
        lcols[part, :] = got[:, rank:]
        return carry

    lax.fori_loop(0, row_tiles, pick, 0)
    kept = jnp.dot(t_ref[...], lcols[...], preferred_element_type=F32)
    kpart[...] = kept.reshape(n, krows, rank)
    pl.semaphore_wait(barrier, n + m - 2)

    def k_copy(d, slot):
        return remote(kpart.at[d], krs.at[slot], k_send.at[d], k_recv.at[slot], "grid", d)

    def g_copy(d, slot):
        return remote(kzag.at[slot], kzag.at[slot], g_send.at[d], g_recv.at[slot], "grid", d)

    core, chip, half = b & 1, b >> 1, m // 2
    mate = b ^ 1
    chip_peers = [lax.rem(chip + o, half) * 2 + core for o in range(1, half)]

    def a_copy(d, slot):
        return remote(kall.at[slot], kall.at[slot], a_send.at[d], a_recv.at[slot], "snap", d)

    def a_forward(slot):
        return remote(kall.at[slot], kall.at[slot], a_send.at[slot ^ 1], a_recv.at[slot], "snap", mate)

    def block(d):
        place = (d & 1) * half + (d >> 1)
        return pl.ds(pl.multiple_of(place * srows, 16), srows)

    def side(which):
        return pl.ds(pl.multiple_of(which * half * srows, 16), half * srows)

    def h_copy(which):
        return remote(spart.at[side(which)], shalf, h_send, h_recv, "snap", mate)

    def s_copy(d, slot):
        return remote(
            spart.at[block(d)], srs.at[slot >> 1], s_send.at[d >> 1], s_recv.at[slot >> 1], "snap", d)

    def f_copy(d, slot):
        return remote(
            sfull.at[block(slot)], sfull.at[block(slot)], f_send.at[d], f_recv.at[slot], "snap", d)

    def f_forward(slot):
        return remote(
            sfull.at[block(slot)], sfull.at[block(slot)], f_send.at[slot ^ 1], f_recv.at[slot],
            "snap", mate)

    def mx_copy(g, d, slot):
        return remote(mx.at[g, slot], mx.at[g, slot], mx_send.at[g, d], mx_recv.at[g, slot], "grid", d)

    for d in z_peers:
        k_copy(d, z).start()
    h_copy(1 - core).start()

    def sketch(g):
        def one(i, carry):
            c = g * per_group + i
            part = pl.ds(pl.multiple_of(c * TILE, TILE), TILE)
            value = jnp.dot(t_ref[...], sv[:, part], preferred_element_type=F32)
            pbuf[c] = value
            mx[g, z, pl.ds(i, 1), :] = jnp.max(jnp.abs(value), axis=0, keepdims=True)
            return carry

        lax.fori_loop(0, per_group, one, 0)
        for d in z_peers:
            mx_copy(g, d, z).start()

    def quantise(g):
        for d in z_peers:
            mx_copy(g, d, d).wait_recv()
        top = mx[g, 0]
        for i in range(1, n):
            top = top + mx[g, i]
        top = jnp.maximum(top, 1e-30)
        scale[g] = top * (1.0 / LIMIT)
        inverse[...] = LIMIT / top

        def one(i, carry):
            c = g * per_group + i
            inv = inverse[pl.ds(i, 1), :]
            q[c] = jnp.floor(pbuf[c] * inv + 0.5).astype(I32).astype(I16)
            return carry

        lax.fori_loop(0, per_group, one, 0)

    def right_copy(c, src):
        return remote(src.at[c], rin.at[c], r_send.at[c], r_recv.at[c], "grid", lax.rem(z + 1, n))

    def left_copy(c, src):
        return remote(src.at[c], lin.at[c], l_send.at[c], l_recv.at[c], "grid", lax.rem(z + n - 1, n))

    def added(x, y):
        return x + y

    def go_right(c):
        right_copy(c, rsum).wait_recv()
        rsum[c] = added(rin[c], q[c])
        right_copy(c, rsum).start()

    def go_left(c):
        left_copy(c, lsum).wait_recv()
        lsum[c] = added(lin[c], q[c])
        left_copy(c, lsum).start()

    def from_ends(g):
        def one(c, carry):
            @pl.when(z == 0)
            def _():
                right_copy(c, q).start()

            @pl.when(z == n - 1)
            def _():
                left_copy(c, q).start()

            return carry

        lax.fori_loop(g * per_group, (g + 1) * per_group, one, 0)

    def flow(step, carry=0):
        @pl.when((z > 0) & (z < n // 2))
        def _():
            @pl.when(step < chunks)
            def _():
                go_right(step)

            @pl.when(step >= LAG)
            def _():
                go_left(step - LAG)

        @pl.when((z >= n // 2) & (z < n - 1))
        def _():
            @pl.when(step < chunks)
            def _():
                go_left(step)

            @pl.when(step >= LAG)
            def _():
                go_right(step - LAG)

        return carry

    def flows(first, last):
        lax.fori_loop(first, last, flow, 0)

    def skeleton_half():
        h_copy(core).wait_recv()
        h_copy(1 - core).wait_send()
        mine = side(core)
        spart[mine, :] = (spart[mine, :].astype(F32) + shalf[...].astype(F32)).astype(BF16)
        for d in chip_peers:
            s_copy(d, b).start()

    def skeleton_block():
        acc = spart[block(b), :].astype(F32)
        for d in chip_peers:
            s_copy(d, d).wait_recv()
            acc = acc + srs[d >> 1].astype(F32)
        sfull[block(b), :] = acc.astype(BF16)
        for d in chip_peers + [mate]:
            f_copy(d, b).start()

    def skeleton_forward():
        for d in chip_peers:
            f_copy(d, d).wait_recv()
            f_forward(d).start()

    def selections():
        def row_of(level, j):
            return mp_ref[pl.ds((m >> (level + 1)) - 1 + j, 1), :]

        ids = [j * 2 * rank + mp_ref[m // 2 - 1 + j:m // 2 + j, :] for j in range(m // 2)]
        for level in range(levels):
            if level:
                merged = []
                for j in range(len(ids) // 2):
                    both = jnp.concatenate([ids[2 * j], ids[2 * j + 1]], axis=1).astype(F32)
                    picker = (
                        lax.broadcasted_iota(I32, (2 * rank, rank), 0)
                        == mp_ref[len(ids) // 2 - 1 + j:len(ids) // 2 + j, :]
                    ).astype(F32)
                    found = precise_dot(jnp.broadcast_to(both, (8, 2 * rank)), picker)
                    merged.append(jnp.floor(found[:1] + 0.5).astype(I32))
                ids = merged
            mine = ids[0]
            for j in range(1, len(ids)):
                mine = jnp.where(b >> (level + 1) == j, ids[j], mine)
            for i in range(m):
                place = lax.broadcasted_iota(I32, (rank, rank), 0) + i * rank
                cpick[i * rank:(i + 1) * rank, level * rank:(level + 1) * rank] = (
                    place == mine).astype(F32).astype(BF16)

    def tree():
        for i in range(m):
            kparts[:, i * rank:(i + 1) * rank] = jnp.concatenate(
                split3(kall[i].reshape(rank, rank)), axis=0)
        three = jnp.dot(kparts[...], cpick[...], preferred_element_type=F32)
        chosen = (three[:rank] + three[rank:2 * rank]) + three[2 * rank:]
        path = [kall[b].reshape(rank, rank)]
        for level in range(levels):
            path.append(chosen[:, level * rank:(level + 1) * rank])
        portions = []
        for level in range(levels):
            row = (m >> (level + 1)) - 1 + (b >> (level + 1))
            picker_t = (
                lax.broadcasted_iota(I32, (rank, rank), 0) + ((b >> level) & 1) * rank
                == mp_ref[pl.ds(row, 1), :]
            ).astype(F32).T
            mask = jnp.sum(picker_t, axis=0, keepdims=True)
            inner = precise_dot(path[level + 1].T, path[level])
            portions.append(precise_dot(mi_ref[row], inner) * (1.0 - mask) + picker_t)
        top = portions[-1]
        for level in range(levels - 2, 0, -1):
            top = precise_dot(top, portions[level])
        first = precise_dot(portions[0], v_s[...])
        composed = precise_dot(top, portions[0]) if levels > 1 else top
        weight = precise_dot(top, first) if levels > 1 else first
        w_hi, w_mid, _ = split3(weight)
        w_s[...] = jnp.concatenate([w_hi, w_hi, w_mid, w_mid], axis=1)
        c_s[...] = composed.astype(BF16)

    def finish(c, carry):
        @pl.when(z == 0)
        def _():
            left_copy(c, lsum).wait_recv()

        @pl.when(z == n - 1)
        def _():
            right_copy(c, rsum).wait_recv()

        g, i = lax.div(c, per_group), lax.rem(c, per_group)
        hit = (lax.broadcasted_iota(I32, (rank, TILE), 1) + c * TILE == pivot_col).astype(F32)
        keep = 1.0 - jnp.sum(hit, axis=0, keepdims=True)
        sums = rin[c].astype(I32) + q[c].astype(I32) + lin[c].astype(I32)
        value = sums.astype(F32) * keep
        hi = value.astype(BF16)
        lo = (value - hi.astype(F32)).astype(BF16)
        mapped = jnp.dot(
            w_s[...], jnp.concatenate([hi, lo, hi, lo], axis=0), preferred_element_type=F32)
        unit = jnp.dot(c_s[...], hit.astype(BF16), preferred_element_type=F32)
        part = pl.ds(pl.multiple_of(c * TILE, TILE), TILE)
        coef_out[:, part] = (mapped * scale[g, pl.ds(i, 1), :] + unit).astype(BF16)
        return carry

    sketch(0)
    sketch(1)
    for d in z_peers:
        k_copy(d, d).wait_recv()
    krs[z] = kpart[z]
    total = krs[0]
    for i in range(1, n):
        total = total + krs[i]
    kzag[z] = total
    for d in z_peers:
        g_copy(d, z).start()
    quantise(0)
    from_ends(0)
    sketch(2)
    quantise(1)
    from_ends(1)
    sketch(3)
    for copy in small[3:]:
        copy.wait()
    for d in z_peers:
        g_copy(d, d).wait_recv()
    kall[b] = kzag[...]
    for d in chip_peers + [mate]:
        a_copy(d, b).start()
    flows(0, 1)
    quantise(2)
    from_ends(2)
    flows(1, 2)
    quantise(3)
    from_ends(3)
    skeleton_half()
    flows(2, 3)
    selections()
    v_s[...] = precise_dot(li_ref[0], kzag[...].reshape(rank, rank).T)
    pivot_col = jnp.broadcast_to(lp_ref[...].astype(F32), (rank, rank)).T[:, :1].astype(I32)
    flows(3, 4)
    for d in chip_peers:
        a_copy(d, d).wait_recv()
        a_forward(d).start()
    flows(4, 5)
    skeleton_block()
    flows(5, 6)
    a_copy(mate, mate).wait_recv()
    for d in chip_peers:
        a_copy(d, d ^ 1).wait_recv()
    tree()
    flows(6, chunks)
    skeleton_forward()
    lax.fori_loop(0, chunks - LAG, finish, 0)
    flows(chunks, chunks + LAG)
    lax.fori_loop(chunks - LAG, chunks, finish, 0)
    f_copy(mate, mate).wait_recv()
    for d in chip_peers:
        f_copy(d, d ^ 1).wait_recv()
    skel_out[...] = sfull[...]

    for d in z_peers:
        k_copy(d, z).wait_send()
        g_copy(d, z).wait_send()
        for g in range(GROUPS):
            mx_copy(g, d, z).wait_send()
    for d in chip_peers:
        s_copy(d, b).wait_send()
        a_copy(d, b).wait_send()
        f_copy(d, b).wait_send()
        a_forward(d).wait_send()
        f_forward(d).wait_send()
    a_copy(mate, b).wait_send()
    f_copy(mate, b).wait_send()

    @pl.when(z < n - 1)
    def _():
        for c in range(chunks):
            right_copy(c, rsum).wait_send()

    @pl.when(z > 0)
    def _():
        for c in range(chunks):
            left_copy(c, lsum).wait_send()


def per_device(
    n, m, snapshots, test_matrix, leaf_pivots, leaf_inverse, merge_pivots, merge_inverse, skeleton_ids
):
    rank = test_matrix.shape[0]
    rows, cols = snapshots.shape
    chunks = cols // TILE
    krows, srows = rank // n, rows // m
    vmem = pl.BlockSpec(memory_space=pltpu.VMEM)
    dma = pltpu.SemaphoreType.DMA
    flow_shape = (chunks, rank, TILE)
    return pl.pallas_call(
        functools.partial(kernel, n, m),
        out_shape=(
            jax.ShapeDtypeStruct((rows, rank), BF16),
            jax.ShapeDtypeStruct((rank, cols), BF16),
        ),
        in_specs=[pl.BlockSpec(memory_space=pl.ANY)] * 7,
        out_specs=(vmem, vmem),
        scratch_shapes=[
            pltpu.VMEM(test_matrix.shape, BF16),
            pltpu.VMEM(leaf_pivots.shape, I32),
            pltpu.VMEM(leaf_inverse.shape, F32),
            pltpu.VMEM(merge_pivots.shape, I32),
            pltpu.VMEM(merge_inverse.shape, F32),
            pltpu.VMEM((1, rank), I32),
            dma((6,)),
            pltpu.VMEM((rows, cols), BF16),
            pltpu.VMEM((cols, 2 * rank), BF16),
            pltpu.VMEM((rows, rank), BF16),
            pltpu.VMEM((rows, rank), BF16),
            pltpu.VMEM((rows // 2, rank), BF16),
            pltpu.VMEM((m // 2, srows, rank), BF16),
            pltpu.VMEM((rows, rank), BF16),
            pltpu.VMEM((n, krows, rank), F32),
            pltpu.VMEM((n, krows, rank), F32),
            pltpu.VMEM((n, krows, rank), F32),
            pltpu.VMEM((m, n, krows, rank), F32),
            pltpu.VMEM((m * rank, rank * (m.bit_length() - 1)), BF16),
            pltpu.VMEM((3 * rank, m * rank), BF16),
            pltpu.VMEM((8, TILE), F32),
            pltpu.VMEM((rank, rank), F32),
            pltpu.VMEM(flow_shape, F32),
            pltpu.VMEM((GROUPS, n, 8, TILE), F32),
            pltpu.VMEM((GROUPS, 8, TILE), F32),
            pltpu.VMEM(flow_shape, I16),
            pltpu.VMEM(flow_shape, I16),
            pltpu.VMEM(flow_shape, I16),
            pltpu.VMEM(flow_shape, I16),
            pltpu.VMEM(flow_shape, I16),
            pltpu.VMEM((rank, 4 * rank), BF16),
            pltpu.VMEM((rank, rank), BF16),
            dma((rows // TILE,)),
            dma((n,)), dma((n,)), dma((n,)), dma((n,)),
            dma((m,)), dma((m,)), dma, dma, dma((m // 2,)), dma((m // 2,)), dma((m,)), dma((m,)),
            dma((GROUPS, n)), dma((GROUPS, n)),
            dma((chunks,)), dma((chunks,)), dma((chunks,)), dma((chunks,)),
        ],
        compiler_params=pltpu.CompilerParams(
            collective_id=0, has_side_effects=True, vmem_limit_bytes=60 * 2**20
        ),
    )(
        snapshots, test_matrix, leaf_pivots, leaf_inverse, merge_pivots, merge_inverse,
        skeleton_ids.reshape(1, rank),
    )


def solution(mesh):
    return jax.shard_map(
        functools.partial(per_device, mesh.shape["grid"], mesh.shape["snap"]),
        mesh=mesh,
        in_specs=(
            P("grid", "snap"),
            P(None, "grid"),
            P("snap", None),
            P("snap", None, None),
            P(),
            P(),
            P(),
        ),
        out_specs=(P("grid", None), P(None, "snap")),
        check_vma=False,
    )
```

```python
import functools

import jax
import jax.numpy as jnp
from jax import lax
from jax.experimental import pallas as pl
from jax.experimental.pallas import tpu as pltpu
from jax.sharding import PartitionSpec as P

PRECISE = lax.Precision.HIGHEST
F32, BF16, I32, I16 = jnp.float32, jnp.bfloat16, jnp.int32, jnp.int16
TILE = 256
LIMIT = 32000.0
LAG = 2
GROUPS = 4
PIECES = 4


def precise_dot(a, b):
    return jnp.dot(a, b, precision=PRECISE, preferred_element_type=F32)


def split3(x):
    hi = x.astype(BF16)
    rest = x - hi.astype(F32)
    mid = rest.astype(BF16)
    lo = (rest - mid.astype(F32)).astype(BF16)
    return hi, mid, lo


def kernel(
    n, m, s_ref, t_hbm, lp_hbm, li_hbm, mp_hbm, mi_hbm, ids_hbm,
    skel_out, coef_out,
    t_ref, lp_ref, li_ref, mp_ref, mi_ref, ids_ref, small_sem,
    sv, oh, spart, lcols, shalf, srs, sfull, kpart, krs, kzag, kall, cpick, kparts, inverse, v_s, pbuf, mx, scale, q, rin, lin, rsum,
    lsum, w_s, c_s,
    load_sem, k_send, k_recv, g_send, g_recv, a_send, a_recv, h_send, h_recv, s_send, s_recv,
    f_send, f_recv,
    mx_send, mx_recv, r_send, r_recv, l_send, l_recv,
):
    z = lax.axis_index("grid")
    b = lax.axis_index("snap")
    rank = t_ref.shape[0]
    rows, cols = sv.shape
    row_tiles, chunks = rows // TILE, cols // TILE
    per_group = chunks // GROUPS
    krows = rank // n
    srows = rows // m
    levels = m.bit_length() - 1

    def remote(src, dst, send, recv, axis, target):
        return pltpu.make_async_remote_copy(
            src_ref=src, dst_ref=dst, send_sem=send, recv_sem=recv,
            device_id={axis: target}, device_id_type=pl.DeviceIdType.MESH,
        )

    def load(i):
        part = pl.ds(pl.multiple_of(i * TILE, TILE), TILE)
        return pltpu.make_async_copy(s_ref.at[part], sv.at[part], load_sem.at[i])

    small = [
        pltpu.make_async_copy(src, dst, small_sem.at[i])
        for i, (src, dst) in enumerate([
            (ids_hbm, ids_ref), (lp_hbm, lp_ref), (t_hbm, t_ref), (mp_hbm, mp_ref),
            (li_hbm, li_ref), (mi_hbm, mi_ref)])
    ]
    for copy in small[:3]:
        copy.start()
    for i in range(row_tiles):
        load(i).start()
    for copy in small[3:]:
        copy.start()

    barrier = pltpu.get_barrier_semaphore()
    z_peers = [lax.rem(z + o, n) for o in range(1, n)]
    b_peers = [lax.rem(b + o, m) for o in range(1, m)]
    for d in z_peers:
        pl.semaphore_signal(barrier, inc=1, device_id={"grid": d}, device_id_type=pl.DeviceIdType.MESH)
    for d in b_peers:
        pl.semaphore_signal(barrier, inc=1, device_id={"snap": d}, device_id_type=pl.DeviceIdType.MESH)

    @pl.when(z == 0)
    def _():
        rin[...] = jnp.zeros_like(rin)

    @pl.when(z == n - 1)
    def _():
        lin[...] = jnp.zeros_like(lin)

    for g in range(GROUPS):
        mx[g, z] = jnp.zeros(mx.shape[2:], F32)

    for copy in small[:2]:
        copy.wait()
    local_ids = ids_ref[...] - b * cols
    picks = jnp.concatenate([local_ids, lp_ref[...]], axis=1)

    def fill(i, carry):
        base = pl.multiple_of(i * TILE, TILE)
        place = lax.broadcasted_iota(I32, (TILE, 2 * rank), 0) + base
        oh[pl.ds(base, TILE), :] = (place == picks).astype(F32).astype(BF16)
        return carry

    lax.fori_loop(0, chunks, fill, 0)
    small[2].wait()

    def pick(i, carry):
        part = pl.ds(pl.multiple_of(i * TILE, TILE), TILE)
        got = jnp.dot(sv[part, :], oh[...], preferred_element_type=F32).astype(BF16)
        spart[part, :] = got[:, :rank]
        lcols[part, :] = got[:, rank:]
        return carry

    for i in range(row_tiles):
        load(i).wait()
    pl.semaphore_wait(barrier, n + m - 2)

    def k_copy(d, slot):
        return remote(kpart.at[d], krs.at[slot], k_send.at[d], k_recv.at[slot], "grid", d)

    def g_copy(d, slot):
        return remote(kzag.at[slot], kzag.at[slot], g_send.at[d], g_recv.at[slot], "grid", d)

    core, chip, half = b & 1, b >> 1, m // 2
    mate = b ^ 1
    chip_peers = [lax.rem(chip + o, half) * 2 + core for o in range(1, half)]

    def a_copy(d, slot):
        return remote(kall.at[slot], kall.at[slot], a_send.at[d], a_recv.at[slot], "snap", d)

    def a_forward(slot):
        return remote(kall.at[slot], kall.at[slot], a_send.at[slot ^ 1], a_recv.at[slot], "snap", mate)

    def block(d):
        place = (d & 1) * half + (d >> 1)
        return pl.ds(pl.multiple_of(place * srows, 16), srows)

    def side(which):
        return pl.ds(pl.multiple_of(which * half * srows, 16), half * srows)

    def h_copy(which):
        return remote(spart.at[side(which)], shalf, h_send, h_recv, "snap", mate)

    def s_copy(d, slot):
        return remote(
            spart.at[block(d)], srs.at[slot >> 1], s_send.at[d >> 1], s_recv.at[slot >> 1], "snap", d)

    def f_copy(d, slot):
        return remote(
            sfull.at[block(slot)], sfull.at[block(slot)], f_send.at[d], f_recv.at[slot], "snap", d)

    def f_forward(slot):
        return remote(
            sfull.at[block(slot)], sfull.at[block(slot)], f_send.at[slot ^ 1], f_recv.at[slot],
            "snap", mate)

    def mx_copy(g, d, slot):
        return remote(mx.at[g, slot], mx.at[g, slot], mx_send.at[g, d], mx_recv.at[g, slot], "grid", d)

    def sketch(g):
        def one(i, carry):
            c = g * per_group + i
            part = pl.ds(pl.multiple_of(c * TILE, TILE), TILE)
            value = jnp.dot(t_ref[...], sv[:, part], preferred_element_type=F32)
            pbuf[c] = value
            mx[g, z, pl.ds(i, 1), :] = jnp.max(jnp.abs(value), axis=0, keepdims=True)
            return carry

        lax.fori_loop(0, per_group, one, 0)
        for d in z_peers:
            mx_copy(g, d, z).start()

    def quantise(g):
        for d in z_peers:
            mx_copy(g, d, d).wait_recv()
        top = mx[g, 0]
        for i in range(1, n):
            top = top + mx[g, i]
        top = jnp.maximum(top, 1e-30)
        scale[g] = top * (1.0 / LIMIT)
        inverse[...] = LIMIT / top

        def one(i, carry):
            c = g * per_group + i
            inv = inverse[pl.ds(i, 1), :]
            q[c] = jnp.floor(pbuf[c] * inv + 0.5).astype(I32).astype(I16)
            return carry

        lax.fori_loop(0, per_group, one, 0)

    def right_copy(c, src):
        return remote(src.at[c], rin.at[c], r_send.at[c], r_recv.at[c], "grid", lax.rem(z + 1, n))

    def left_copy(c, src):
        return remote(src.at[c], lin.at[c], l_send.at[c], l_recv.at[c], "grid", lax.rem(z + n - 1, n))

    def added(x, y):
        return x + y

    def go_right(c):
        right_copy(c, rsum).wait_recv()
        rsum[c] = added(rin[c], q[c])
        right_copy(c, rsum).start()

    def go_left(c):
        left_copy(c, lsum).wait_recv()
        lsum[c] = added(lin[c], q[c])
        left_copy(c, lsum).start()

    def from_ends(g):
        def one(c, carry):
            @pl.when(z == 0)
            def _():
                right_copy(c, q).start()

            @pl.when(z == n - 1)
            def _():
                left_copy(c, q).start()

            return carry

        lax.fori_loop(g * per_group, (g + 1) * per_group, one, 0)

    def flow(step, carry=0):
        @pl.when((z > 0) & (z < n // 2))
        def _():
            @pl.when(step < chunks)
            def _():
                go_right(step)

            @pl.when(step >= LAG)
            def _():
                go_left(step - LAG)

        @pl.when((z >= n // 2) & (z < n - 1))
        def _():
            @pl.when(step < chunks)
            def _():
                go_left(step)

            @pl.when(step >= LAG)
            def _():
                go_right(step - LAG)

        return carry

    def flows(first, last):
        lax.fori_loop(first, last, flow, 0)

    def skeleton_half():
        h_copy(core).wait_recv()
        h_copy(1 - core).wait_send()
        mine = side(core)
        spart[mine, :] = (spart[mine, :].astype(F32) + shalf[...].astype(F32)).astype(BF16)
        for d in chip_peers:
            s_copy(d, b).start()

    def skeleton_block():
        acc = spart[block(b), :].astype(F32)
        for d in chip_peers:
            s_copy(d, d).wait_recv()
            acc = acc + srs[d >> 1].astype(F32)
        sfull[block(b), :] = acc.astype(BF16)
        for d in chip_peers + [mate]:
            f_copy(d, b).start()

    def skeleton_forward():
        for d in chip_peers:
            f_copy(d, d).wait_recv()
            f_forward(d).start()

    def selections():
        def row_of(level, j):
            return mp_ref[pl.ds((m >> (level + 1)) - 1 + j, 1), :]

        ids = [j * 2 * rank + mp_ref[m // 2 - 1 + j:m // 2 + j, :] for j in range(m // 2)]
        for level in range(levels):
            if level:
                merged = []
                for j in range(len(ids) // 2):
                    both = jnp.concatenate([ids[2 * j], ids[2 * j + 1]], axis=1).astype(F32)
                    picker = (
                        lax.broadcasted_iota(I32, (2 * rank, rank), 0)
                        == mp_ref[len(ids) // 2 - 1 + j:len(ids) // 2 + j, :]
                    ).astype(F32)
                    found = precise_dot(jnp.broadcast_to(both, (8, 2 * rank)), picker)
                    merged.append(jnp.floor(found[:1] + 0.5).astype(I32))
                ids = merged
            mine = ids[0]
            for j in range(1, len(ids)):
                mine = jnp.where(b >> (level + 1) == j, ids[j], mine)
            for i in range(m):
                place = lax.broadcasted_iota(I32, (rank, rank), 0) + i * rank
                cpick[i * rank:(i + 1) * rank, level * rank:(level + 1) * rank] = (
                    place == mine).astype(F32).astype(BF16)

    def tree():
        for i in range(m):
            kparts[:, i * rank:(i + 1) * rank] = jnp.concatenate(
                split3(kall[i].reshape(rank, rank)), axis=0)
        three = jnp.dot(kparts[...], cpick[...], preferred_element_type=F32)
        chosen = (three[:rank] + three[rank:2 * rank]) + three[2 * rank:]
        path = [kall[b].reshape(rank, rank)]
        for level in range(levels):
            path.append(chosen[:, level * rank:(level + 1) * rank])
        portions = []
        for level in range(levels):
            row = (m >> (level + 1)) - 1 + (b >> (level + 1))
            picker_t = (
                lax.broadcasted_iota(I32, (rank, rank), 0) + ((b >> level) & 1) * rank
                == mp_ref[pl.ds(row, 1), :]
            ).astype(F32).T
            mask = jnp.sum(picker_t, axis=0, keepdims=True)
            inner = precise_dot(path[level + 1].T, path[level])
            portions.append(precise_dot(mi_ref[row], inner) * (1.0 - mask) + picker_t)
        top = portions[-1]
        for level in range(levels - 2, 0, -1):
            top = precise_dot(top, portions[level])
        first = precise_dot(portions[0], v_s[...])
        composed = precise_dot(top, portions[0]) if levels > 1 else top
        weight = precise_dot(top, first) if levels > 1 else first
        w_hi, w_mid, _ = split3(weight)
        w_s[...] = jnp.concatenate([w_hi, w_hi, w_mid, w_mid], axis=1)
        c_s[...] = composed.astype(BF16)

    def finish(c, carry):
        @pl.when(z == 0)
        def _():
            left_copy(c, lsum).wait_recv()

        @pl.when(z == n - 1)
        def _():
            right_copy(c, rsum).wait_recv()

        g, i = lax.div(c, per_group), lax.rem(c, per_group)
        hit = (lax.broadcasted_iota(I32, (rank, TILE), 1) + c * TILE == pivot_col).astype(F32)
        keep = 1.0 - jnp.sum(hit, axis=0, keepdims=True)
        sums = rin[c].astype(I32) + q[c].astype(I32) + lin[c].astype(I32)
        value = sums.astype(F32) * keep
        hi = value.astype(BF16)
        lo = (value - hi.astype(F32)).astype(BF16)
        mapped = jnp.dot(
            w_s[...], jnp.concatenate([hi, lo, hi, lo], axis=0), preferred_element_type=F32)
        unit = jnp.dot(c_s[...], hit.astype(BF16), preferred_element_type=F32)
        part = pl.ds(pl.multiple_of(c * TILE, TILE), TILE)
        coef_out[:, part] = (mapped * scale[g, pl.ds(i, 1), :] + unit).astype(BF16)
        return carry

    sketch(0)
    sketch(1)
    lax.fori_loop(0, row_tiles // 2, pick, 0)
    quantise(0)
    from_ends(0)
    quantise(1)
    from_ends(1)
    lax.fori_loop(row_tiles // 2, row_tiles, pick, 0)
    kept = jnp.dot(t_ref[...], lcols[...], preferred_element_type=F32)
    kpart[...] = kept.reshape(n, krows, rank)
    for d in z_peers:
        k_copy(d, z).start()
    h_copy(1 - core).start()
    flows(0, 2)
    sketch(2)
    for d in z_peers:
        k_copy(d, d).wait_recv()
    krs[z] = kpart[z]
    total = krs[0]
    for i in range(1, n):
        total = total + krs[i]
    kzag[z] = total
    for d in z_peers:
        g_copy(d, z).start()
    sketch(3)
    flows(2, 3)
    quantise(2)
    from_ends(2)
    quantise(3)
    from_ends(3)
    for copy in small[3:]:
        copy.wait()
    for d in z_peers:
        g_copy(d, d).wait_recv()
    kall[b] = kzag[...]
    for d in chip_peers + [mate]:
        a_copy(d, b).start()
    flows(3, 4)
    skeleton_half()
    selections()
    v_s[...] = precise_dot(li_ref[0], kzag[...].reshape(rank, rank).T)
    pivot_col = jnp.broadcast_to(lp_ref[...].astype(F32), (rank, rank)).T[:, :1].astype(I32)
    flows(4, 5)
    for d in chip_peers:
        a_copy(d, d).wait_recv()
        a_forward(d).start()
    flows(5, 6)
    skeleton_block()
    a_copy(mate, mate).wait_recv()
    for d in chip_peers:
        a_copy(d, d ^ 1).wait_recv()
    tree()
    flows(6, chunks)
    skeleton_forward()
    lax.fori_loop(0, chunks - LAG, finish, 0)
    flows(chunks, chunks + LAG)
    lax.fori_loop(chunks - LAG, chunks, finish, 0)
    f_copy(mate, mate).wait_recv()
    for d in chip_peers:
        f_copy(d, d ^ 1).wait_recv()
    skel_out[...] = sfull[...]

    for d in z_peers:
        k_copy(d, z).wait_send()
        g_copy(d, z).wait_send()
        for g in range(GROUPS):
            mx_copy(g, d, z).wait_send()
    for d in chip_peers:
        s_copy(d, b).wait_send()
        a_copy(d, b).wait_send()
        f_copy(d, b).wait_send()
        a_forward(d).wait_send()
        f_forward(d).wait_send()
    a_copy(mate, b).wait_send()
    f_copy(mate, b).wait_send()

    @pl.when(z < n - 1)
    def _():
        for c in range(chunks):
            right_copy(c, rsum).wait_send()

    @pl.when(z > 0)
    def _():
        for c in range(chunks):
            left_copy(c, lsum).wait_send()


def hand_over(skel_in, coef_in, skel_out, coef_out, sems):
    copies = []
    for k, (src, dst) in enumerate([(skel_in, skel_out), (coef_in, coef_out)]):
        step = src.shape[0] // PIECES
        for i in range(PIECES):
            part = pl.ds(i * step, step)
            copies.append(pltpu.make_async_copy(src.at[part], dst.at[part], sems.at[k, i]))
    for copy in copies:
        copy.start()
    for copy in copies:
        copy.wait()


def per_device(
    n, m, snapshots, test_matrix, leaf_pivots, leaf_inverse, merge_pivots, merge_inverse, skeleton_ids
):
    rank = test_matrix.shape[0]
    rows, cols = snapshots.shape
    chunks = cols // TILE
    krows, srows = rank // n, rows // m
    vmem = pl.BlockSpec(memory_space=pltpu.VMEM)
    dma = pltpu.SemaphoreType.DMA
    flow_shape = (chunks, rank, TILE)
    shapes = (
        jax.ShapeDtypeStruct((rows, rank), BF16),
        jax.ShapeDtypeStruct((rank, cols), BF16),
    )
    outs = pl.pallas_call(
        functools.partial(kernel, n, m),
        out_shape=shapes,
        in_specs=[pl.BlockSpec(memory_space=pl.ANY)] * 7,
        out_specs=(vmem, vmem),
        scratch_shapes=[
            pltpu.VMEM(test_matrix.shape, BF16),
            pltpu.VMEM(leaf_pivots.shape, I32),
            pltpu.VMEM(leaf_inverse.shape, F32),
            pltpu.VMEM(merge_pivots.shape, I32),
            pltpu.VMEM(merge_inverse.shape, F32),
            pltpu.VMEM((1, rank), I32),
            dma((6,)),
            pltpu.VMEM((rows, cols), BF16),
            pltpu.VMEM((cols, 2 * rank), BF16),
            pltpu.VMEM((rows, rank), BF16),
            pltpu.VMEM((rows, rank), BF16),
            pltpu.VMEM((rows // 2, rank), BF16),
            pltpu.VMEM((m // 2, srows, rank), BF16),
            pltpu.VMEM((rows, rank), BF16),
            pltpu.VMEM((n, krows, rank), F32),
            pltpu.VMEM((n, krows, rank), F32),
            pltpu.VMEM((n, krows, rank), F32),
            pltpu.VMEM((m, n, krows, rank), F32),
            pltpu.VMEM((m * rank, rank * (m.bit_length() - 1)), BF16),
            pltpu.VMEM((3 * rank, m * rank), BF16),
            pltpu.VMEM((8, TILE), F32),
            pltpu.VMEM((rank, rank), F32),
            pltpu.VMEM(flow_shape, F32),
            pltpu.VMEM((GROUPS, n, 8, TILE), F32),
            pltpu.VMEM((GROUPS, 8, TILE), F32),
            pltpu.VMEM(flow_shape, I16),
            pltpu.VMEM(flow_shape, I16),
            pltpu.VMEM(flow_shape, I16),
            pltpu.VMEM(flow_shape, I16),
            pltpu.VMEM(flow_shape, I16),
            pltpu.VMEM((rank, 4 * rank), BF16),
            pltpu.VMEM((rank, rank), BF16),
            dma((rows // TILE,)),
            dma((n,)), dma((n,)), dma((n,)), dma((n,)),
            dma((m,)), dma((m,)), dma, dma, dma((m // 2,)), dma((m // 2,)), dma((m,)), dma((m,)),
            dma((GROUPS, n)), dma((GROUPS, n)),
            dma((chunks,)), dma((chunks,)), dma((chunks,)), dma((chunks,)),
        ],
        compiler_params=pltpu.CompilerParams(
            collective_id=0, has_side_effects=True, vmem_limit_bytes=60 * 2**20
        ),
    )(
        snapshots, test_matrix, leaf_pivots, leaf_inverse, merge_pivots, merge_inverse,
        skeleton_ids.reshape(1, rank),
    )
    anywhere = pl.BlockSpec(memory_space=pl.ANY)
    return pl.pallas_call(
        hand_over,
        out_shape=shapes,
        in_specs=[anywhere] * 2,
        out_specs=(anywhere,) * 2,
        scratch_shapes=[dma((2, PIECES))],
        compiler_params=pltpu.CompilerParams(vmem_limit_bytes=60 * 2**20),
    )(*outs)


def solution(mesh):
    return jax.shard_map(
        functools.partial(per_device, mesh.shape["grid"], mesh.shape["snap"]),
        mesh=mesh,
        in_specs=(
            P("grid", "snap"),
            P(None, "grid"),
            P("snap", None),
            P("snap", None, None),
            P(),
            P(),
            P(),
        ),
        out_specs=(P("grid", None), P(None, "snap")),
        check_vma=False,
    )
```
